512 devices in a mesh: resp: 64 (over y, x, z_hi), head: 8 (over z_lo, core).
Axes of the slice: x: 4, y: 8, z: 8 (z_hi: 2, z_lo: 4; z = z_hi * 4 + z_lo), core: 2. Of those that a mesh axis runs over, the one named last changes fastest.
Arguments:
- queries: bfloat16 [16384, 8192], P(('resp', 'head')), may hold values from -6 to 6
- resp_keys: bfloat16 [16384, 1024], P(('resp', 'head')), may hold values from -6 to 6
- resp_values: bfloat16 [16384, 1024], P(('resp', 'head')), may hold values from -6 to 6
- out_grad: bfloat16 [16384, 8192], P(('resp', 'head')), may hold values from -6 to 6
- prompt_keys: bfloat16 [1024, 1024], P(('resp', 'head')), may hold values from -10 to 10
- prompt_values: bfloat16 [1024, 1024], P(('resp', 'head')), may hold values from -6 to 6
- lengths: int32 [64, 4], P('resp'), may hold values from 1 to 160, 256 in all within a row
Outputs:
- attention: bfloat16 [16384, 8192], P(('resp', 'head'))
- query_grad: bfloat16 [16384, 8192], P(('resp', 'head'))
- resp_key_grad: bfloat16 [16384, 1024], P(('resp', 'head'))
- resp_value_grad: bfloat16 [16384, 1024], P(('resp', 'head'))
- prompt_key_grad: float32 [1024, 1024], P(('resp', 'head'))
- prompt_value_grad: float32 [1024, 1024], P(('resp', 'head'))
The draws below stay inside these ranges and needn't reach their ends.
All inputs are finite; a program needn't handle non-finite values.
Results may differ from the reference program's by a relative error of at most 0.035.
Values may be sent and summed in bfloat16 or wider, within the bound.
No kernel may reach another device: no remote copies, remote signals or barrier semaphores. Data moves between devices by JAX's collectives and lax.ppermute only.
A program may use at most 64 MiB of HBM per device.

```python
import math
import jax
import jax.numpy as jnp
import numpy as np
from jax import lax

QH = 64
KVH = 8
DH = 128
CAP = 256
SLOTS = 4
MOST = 160
RTOK = 16384
PROMPT_TOK = 1024
N_RESP = 64


def draw_queries(key, part):
    key = jax.random.fold_in(key, 11)
    shape = (RTOK, QH * DH)
    base = jnp.clip(jax.random.normal(key, shape, jnp.float32), -4.0, 4.0)
    return base.astype(jnp.bfloat16)


def draw_prompt_keys(key, part):
    key = jax.random.fold_in(key, 23)
    shape = (PROMPT_TOK, KVH * DH)
    base = jnp.clip(jax.random.normal(key, shape, jnp.float32), -4.0, 4.0)
    return base.astype(jnp.bfloat16)


def steps_of(stream_key, extent, pieces, least, top_value):
    factor_of = 1.0
    for dim, blocks in pieces:
        draws = jax.random.uniform(jax.random.fold_in(jax.random.fold_in(stream_key, 6), dim), (blocks,), jnp.float32, least / len(pieces), top_value / len(pieces))
        factor_of = factor_of * jnp.repeat(jnp.exp(draws), extent[dim] // blocks).reshape((-1,) + (1,) * (len(extent) - 1 - dim))
    return factor_of


def profile(count, total, most, slope):
    portions = [(1 << 20) // math.isqrt(standing ** slope) + 1 for standing in range(2, count + 1)]
    spare, holding = total - most - (count - 1), [1] * (count - 1)
    while spare > 0:
        candidates = [i for i in range(count - 1) if holding[i] < most]
        whole, left = sum([portions[i] for i in candidates]), spare
        for i in candidates:
            addition = min(most - holding[i], max(1, left * portions[i] // whole), spare)
            holding[i] = holding[i] + addition
            spare = spare - addition
    return np.array([most] + holding)


def uneven(rng, number_of, total, bound, skew):
    if number_of == 2:
        one = jax.random.randint(rng, (), max(1, total - bound), min(bound, total - 1) + 1)
        return jnp.stack([one, total - one])
    tallies = jnp.asarray(profile(number_of, total, bound, skew), jnp.int32)
    pairs = (number_of - 1) // 2
    donor, sink = tallies[1:1 + 2 * pairs:2], tallies[2:2 + 2 * pairs:2]
    room = jnp.minimum(donor - 1, bound - sink)
    moved = jax.random.randint(jax.random.fold_in(rng, 1), (pairs,), 0, 1 << 20) % (room + 1)
    tallies = tallies.at[1:1 + 2 * pairs:2].set(donor - moved).at[2:2 + 2 * pairs:2].set(sink + moved)
    return tallies[jax.random.permutation(jax.random.fold_in(rng, 2), number_of)]


def scatter_about(rng, extent, deviation, reach, pieces=(), kind=jnp.bfloat16):
    gain = steps_of(rng, extent, pieces, -0.22, 0.18) if pieces else 1.0
    result = jax.random.normal(rng, extent, jnp.float32) * deviation * gain
    return jnp.minimum(jnp.maximum(result, -reach), reach).astype(kind)


def setup_inputs(seed: int = 0) -> dict:
    arg_keys = jax.random.split(jax.random.key(seed), 8)
    queries = draw_queries(jax.random.fold_in(arg_keys[7], 71), 0)
    resp_keys = scatter_about(arg_keys[1], (RTOK, KVH * DH), 1.0, 6.0, ((0, 512),))
    resp_values = scatter_about(arg_keys[2], (RTOK, KVH * DH), 1.0, 6.0, ((0, 512),))
    out_grad = scatter_about(arg_keys[3], (RTOK, QH * DH), 1.0, 6.0, ((0, 512),))
    prompt_keys = draw_prompt_keys(jax.random.fold_in(arg_keys[7], 71), 0)
    prompt_values = scatter_about(arg_keys[5], (PROMPT_TOK, KVH * DH), 1.0, 6.0, ((0, 512),))
    lengths = jax.vmap(lambda own: uneven(own, SLOTS, CAP, MOST, 2))(jax.random.split(arg_keys[6], N_RESP)).reshape((N_RESP, SLOTS)).astype(jnp.int32)
    return {"queries": queries, "resp_keys": resp_keys, "resp_values": resp_values, "out_grad": out_grad, "prompt_keys": prompt_keys, "prompt_values": prompt_values, "lengths": lengths}


def response_mask(seg_lengths, buffer_rows):
    seg_ends = jnp.cumsum(seg_lengths).astype(jnp.int32)
    positions = jnp.arange(buffer_rows, dtype=jnp.int32)
    starts = lax.optimization_barrier(jnp.max(jnp.where(seg_ends[None, :] <= positions[:, None], seg_ends[None, :], 0), axis=1))
    return (positions[None, :] >= starts[:, None]) & (positions[None, :] <= positions[:, None])

def to_rows(blocks):
    return blocks.transpose(2, 0, 1, 3).reshape(CAP, QH * DH)

def reference(queries, resp_keys, resp_values, out_grad, prompt_keys, prompt_values, lengths):
    score_scale = 1.0 / math.sqrt(DH)
    group_size = QH // KVH
    prompt_k = prompt_keys.reshape(PROMPT_TOK, KVH, DH).transpose(1, 0, 2).astype(jnp.float32)
    prompt_v = prompt_values.reshape(PROMPT_TOK, KVH, DH).transpose(1, 0, 2).astype(jnp.float32)

    def one_buffer(totals, sliced):
        q_rows, k_rows, v_rows, g_rows, seg_lengths = sliced
        query_h = q_rows.reshape(CAP, KVH, group_size, DH).transpose(1, 2, 0, 3).astype(jnp.float32)
        grad_h = g_rows.reshape(CAP, KVH, group_size, DH).transpose(1, 2, 0, 3).astype(jnp.float32)
        key_h = jnp.concatenate([prompt_k, k_rows.reshape(CAP, KVH, DH).transpose(1, 0, 2).astype(jnp.float32)], axis=1)
        value_h = jnp.concatenate([prompt_v, v_rows.reshape(CAP, KVH, DH).transpose(1, 0, 2).astype(jnp.float32)], axis=1)
        key_mask = jnp.concatenate([jnp.ones((CAP, PROMPT_TOK), dtype=jnp.bool_), response_mask(seg_lengths, CAP)], axis=1)
        scores = jnp.einsum('hgtd,hkd->hgtk', query_h, key_h) * score_scale
        scores = jnp.where(key_mask[None, None], scores, -jnp.inf)
        row_peak = lax.optimization_barrier(jnp.max(scores, axis=-1, keepdims=True))
        exp_terms = jnp.exp(scores - row_peak)
        weights = exp_terms / lax.optimization_barrier(jnp.sum(exp_terms, axis=-1, keepdims=True))
        weights_bf = lax.optimization_barrier(weights.astype(jnp.bfloat16)).astype(jnp.float32)
        head_out = jnp.einsum('hgtk,hkd->hgtd', weights_bf, value_h).astype(jnp.bfloat16)
        out_wide = lax.optimization_barrier(head_out).astype(jnp.float32)
        out_delta = lax.optimization_barrier(jnp.sum(grad_h * out_wide, axis=-1, keepdims=True))
        dweights = jnp.einsum('hgtd,hkd->hgtk', grad_h, value_h)
        dscores = lax.optimization_barrier((weights * (dweights - out_delta)).astype(jnp.bfloat16)).astype(jnp.float32)
        query_grad = (jnp.einsum('hgtk,hkd->hgtd', dscores, key_h) * score_scale).astype(jnp.bfloat16)
        key_grad = jnp.einsum('hgtk,hgtd->hkd', dscores, query_h) * score_scale
        value_grad = jnp.einsum('hgtk,hgtd->hkd', weights_bf, grad_h)
        total_k, total_v = totals
        total_k = total_k + key_grad[:, :PROMPT_TOK]
        total_v = total_v + value_grad[:, :PROMPT_TOK]
        own_k = key_grad[:, PROMPT_TOK:].transpose(1, 0, 2).reshape(CAP, KVH * DH).astype(jnp.bfloat16)
        own_v = value_grad[:, PROMPT_TOK:].transpose(1, 0, 2).reshape(CAP, KVH * DH).astype(jnp.bfloat16)
        return ((total_k, total_v), (to_rows(head_out), to_rows(query_grad), own_k, own_v))
    sliced = (queries.reshape(N_RESP, CAP, QH * DH), resp_keys.reshape(N_RESP, CAP, KVH * DH), resp_values.reshape(N_RESP, CAP, KVH * DH), out_grad.reshape(N_RESP, CAP, QH * DH), lengths)
    start = (jnp.zeros((KVH, PROMPT_TOK, DH), jnp.float32), jnp.zeros((KVH, PROMPT_TOK, DH), jnp.float32))
    totals, stacked = lax.scan(one_buffer, start, sliced)
    attention, query_grad, key_part, value_part = stacked
    prompt_key_grad = totals[0].transpose(1, 0, 2).reshape(PROMPT_TOK, KVH * DH)
    prompt_value_grad = totals[1].transpose(1, 0, 2).reshape(PROMPT_TOK, KVH * DH)
    return (attention.reshape(RTOK, QH * DH), query_grad.reshape(RTOK, QH * DH), key_part.reshape(RTOK, KVH * DH), value_part.reshape(RTOK, KVH * DH), prompt_key_grad, prompt_value_grad)
```

```python
import functools
import math

import jax
import jax.numpy as jnp
from jax import lax
from jax.experimental import pallas as pl
from jax.experimental.pallas import tpu as pltpu
from jax.sharding import Mesh, PartitionSpec as P

DH = 128
AXES = ("y", "x", "z_hi", "z_lo", "core")
ROW_AXES = ("y", "x")
Z_AXES = ("z_hi", "z_lo", "core")
HEAD_AXES = ("z_lo", "core")
PEERS = 8
SLOTS = 4
ROWS = 32
GROUP = 8
QCOLS = GROUP * DH
BLOCK_COLS = 2 * QCOLS + 2 * DH
OWN = PEERS * ROWS
PLACES = 32
PROMPT = PLACES * 32
KEYS = PROMPT + OWN
CHUNK = 256
SCALE = 1.0 / math.sqrt(DH)
EXP2_SCALE = SCALE * math.log2(math.e)
ANY = pl.BlockSpec(memory_space=pl.ANY)
SMEM = pl.BlockSpec(memory_space=pltpu.SMEM)


def cut_at(peer):
    wide = pl.ds(pl.multiple_of(peer * QCOLS, QCOLS), QCOLS)
    narrow = pl.ds(pl.multiple_of(peer * DH, DH), DH)
    return (
        (wide, pl.ds(0, QCOLS)),
        (wide, pl.ds(QCOLS, QCOLS)),
        (narrow, pl.ds(2 * QCOLS, DH)),
        (narrow, pl.ds(2 * QCOLS + DH, DH)),
    )


def pack_kernel(me_ref, q_ref, g_ref, k_ref, v_ref, *rest):
    outs, sems = rest[:PEERS], rest[PEERS]
    copies = []
    for s in range(PEERS):
        peer = me_ref[0] ^ s
        for n, (src, (here, there)) in enumerate(zip((q_ref, g_ref, k_ref, v_ref), cut_at(peer))):
            copies.append(
                pltpu.make_async_copy(src.at[:, here], outs[s].at[:, there], sems.at[s * 4 + n])
            )
    for copy in copies:
        copy.start()
    for copy in copies:
        copy.wait()


def unpack_kernel(me_ref, *rest):
    blocks, outs, sems = rest[:PEERS], rest[PEERS : PEERS + 4], rest[PEERS + 4]
    copies = []
    for s in range(PEERS):
        peer = me_ref[0] ^ s
        for n, (dst, (here, there)) in enumerate(zip(outs, cut_at(peer))):
            copies.append(
                pltpu.make_async_copy(blocks[s].at[:, there], dst.at[:, here], sems.at[s * 4 + n])
            )
    for copy in copies:
        copy.start()
    for copy in copies:
        copy.wait()


def attend_kernel(me_ref, len_ref, prompt_ref, *rest):
    blocks = rest[:PEERS]
    outs = rest[PEERS : 2 * PEERS]
    (
        prompt_out, held, prompt_held, keys, values, keys_t, values_t,
        dkeys, dvalues, s_ref, p_ref, d_ref, made, prompt_made, sems, out_sems,
    ) = rest[2 * PEERS :]
    me = me_ref[0]
    ins = [pltpu.make_async_copy(prompt_ref, prompt_held, sems.at[PEERS])]
    for s in range(PEERS):
        ins.append(pltpu.make_async_copy(blocks[s], held.at[me ^ s], sems.at[s]))
    for copy in ins:
        copy.start()
    for copy in ins:
        copy.wait()
    for n, (natural, turned) in enumerate(((keys, keys_t), (values, values_t))):
        natural[:PROMPT, :] = prompt_held[:, n].reshape(PROMPT, DH)
        natural[PROMPT:, :] = held[:, :, 2 * QCOLS + n * DH : 2 * QCOLS + (n + 1) * DH].reshape(OWN, DH)
        for c in range(KEYS // CHUNK):
            turned[:, c * CHUNK : (c + 1) * CHUNK] = natural[c * CHUNK : (c + 1) * CHUNK, :].T
    dkeys[...] = jnp.zeros_like(dkeys)
    dvalues[...] = jnp.zeros_like(dvalues)
    ends = []
    total = jnp.int32(0)
    for n in range(SLOTS):
        total = total + len_ref[0, n]
        ends.append(total)
    lanes = lax.broadcasted_iota(jnp.int32, (1, GROUP * ROWS), 1)
    key_at = lax.broadcasted_iota(jnp.int32, (OWN, GROUP * ROWS), 0)
    chunks = [slice(c * CHUNK, (c + 1) * CHUNK) for c in range(KEYS // CHUNK)]

    def one_block(j, carry):
        q = jnp.concatenate([held[j, :, h * DH : (h + 1) * DH] for h in range(GROUP)], axis=0)
        g = jnp.concatenate(
            [held[j, :, QCOLS + h * DH : QCOLS + (h + 1) * DH] for h in range(GROUP)], axis=0
        )
        q_t, g_t = q.T, g.T
        row = j * ROWS + (lanes & (ROWS - 1))
        first = jnp.zeros_like(row)
        for end in ends:
            first = jnp.maximum(first, jnp.where(end <= row, end, 0))
        seen = (key_at >= first) & (key_at <= row)
        peak = jnp.full((8, GROUP * ROWS), -jnp.inf, jnp.float32)
        for c in chunks:
            s = jnp.dot(keys[c, :], q_t, preferred_element_type=jnp.float32)
            if c.start >= PROMPT:
                s = jnp.where(seen, s, -jnp.inf)
            s_ref[c, :] = s
            peak = jnp.maximum(peak, jnp.max(s.reshape(CHUNK // 8, 8, GROUP * ROWS), axis=0))
        peak = jnp.max(peak, axis=0, keepdims=True) * EXP2_SCALE
        norm = jnp.zeros((8, GROUP * ROWS), jnp.float32)
        for c in chunks:
            e = jnp.exp2(s_ref[c, :] * EXP2_SCALE - peak)
            s_ref[c, :] = e
            norm = norm + jnp.sum(e.reshape(CHUNK // 8, 8, GROUP * ROWS), axis=0)
        inverse = 1.0 / jnp.sum(norm, axis=0, keepdims=True)
        for c in chunks:
            w = s_ref[c, :] * inverse
            s_ref[c, :] = w
            w = w.astype(jnp.bfloat16)
            p_ref[c, :] = w
            dvalues[c, :] += jnp.dot(w, g, preferred_element_type=jnp.float32)
        out_t = jnp.dot(values_t[...], p_ref[...], preferred_element_type=jnp.float32)
        out_t = out_t.astype(jnp.bfloat16)
        delta = jnp.sum(
            g_t.astype(jnp.float32) * out_t.astype(jnp.float32), axis=0, keepdims=True
        )
        for c in chunks:
            dw = jnp.dot(values[c, :], g_t, preferred_element_type=jnp.float32)
            ds = (s_ref[c, :] * (dw - delta)).astype(jnp.bfloat16)
            d_ref[c, :] = ds
            dkeys[c, :] += jnp.dot(ds, q, preferred_element_type=jnp.float32)
        dq_t = jnp.dot(keys_t[...], d_ref[...], preferred_element_type=jnp.float32) * SCALE
        out = out_t.T
        dq = dq_t.astype(jnp.bfloat16).T
        for h in range(GROUP):
            made[j, :, h * DH : (h + 1) * DH] = out[h * ROWS : (h + 1) * ROWS, :]
            made[j, :, QCOLS + h * DH : QCOLS + (h + 1) * DH] = dq[h * ROWS : (h + 1) * ROWS, :]
        return carry

    lax.fori_loop(0, PEERS, one_block, 0)
    for n, (grads, factor) in enumerate(((dkeys, SCALE), (dvalues, 1.0))):
        prompt_made[:, n] = (
            (grads[:PROMPT, :] * factor).astype(jnp.bfloat16).reshape(PLACES, PROMPT // PLACES, DH)
        )
        made[:, :, 2 * QCOLS + n * DH : 2 * QCOLS + (n + 1) * DH] = (
            (grads[PROMPT:, :] * factor).astype(jnp.bfloat16).reshape(PEERS, ROWS, DH)
        )
    backs = [pltpu.make_async_copy(prompt_made, prompt_out, out_sems.at[PEERS])]
    for s in range(PEERS):
        backs.append(pltpu.make_async_copy(made.at[me ^ s], outs[s], out_sems.at[s]))
    for copy in backs:
        copy.start()
    for copy in backs:
        copy.wait()


def exchange(blocks):
    moved = [blocks[0]]
    for s in range(1, PEERS):
        moved.append(lax.ppermute(blocks[s], HEAD_AXES, [(i, i ^ s) for i in range(PEERS)]))
    return moved


def on_device(queries, resp_keys, resp_values, out_grad, prompt_keys, prompt_values, lengths):
    bf16 = jnp.bfloat16
    me = lax.axis_index(HEAD_AXES).astype(jnp.int32).reshape(1)
    block = jax.ShapeDtypeStruct((ROWS, BLOCK_COLS), bf16)
    own_rows = prompt_keys.shape[0]

    by_head = jnp.stack(
        [prompt_keys.reshape(own_rows, PEERS, DH), prompt_values.reshape(own_rows, PEERS, DH)]
    ).transpose(2, 0, 1, 3)
    by_head = jnp.broadcast_to(by_head[None], (2,) + by_head.shape).reshape(16, 2, own_rows, DH)
    line = lax.all_to_all(by_head, Z_AXES, split_axis=0, concat_axis=0, tiled=True)
    line = line.transpose(1, 0, 2, 3).reshape(2, 16 * own_rows, DH)
    spread = jnp.broadcast_to(line[None], (PLACES,) + line.shape)
    prompt = lax.all_to_all(spread, ROW_AXES, split_axis=0, concat_axis=0, tiled=True)

    packed = pl.pallas_call(
        pack_kernel,
        out_shape=[block] * PEERS,
        in_specs=[SMEM] + [ANY] * 4,
        out_specs=[ANY] * PEERS,
        scratch_shapes=[pltpu.SemaphoreType.DMA((4 * PEERS,))],
        name="pack",
    )(me, queries, out_grad, resp_keys, resp_values)
    held = exchange(packed)

    width = GROUP * ROWS
    made = pl.pallas_call(
        attend_kernel,
        out_shape=[block] * PEERS + [jax.ShapeDtypeStruct(prompt.shape, bf16)],
        in_specs=[SMEM, SMEM] + [ANY] * (PEERS + 1),
        out_specs=[ANY] * (PEERS + 1),
        scratch_shapes=[
            pltpu.VMEM((PEERS, ROWS, BLOCK_COLS), bf16),
            pltpu.VMEM((PLACES, 2, PROMPT // PLACES, DH), bf16),
            pltpu.VMEM((KEYS, DH), bf16),
            pltpu.VMEM((KEYS, DH), bf16),
            pltpu.VMEM((DH, KEYS), bf16),
            pltpu.VMEM((DH, KEYS), bf16),
            pltpu.VMEM((KEYS, DH), jnp.float32),
            pltpu.VMEM((KEYS, DH), jnp.float32),
            pltpu.VMEM((KEYS, width), jnp.float32),
            pltpu.VMEM((KEYS, width), bf16),
            pltpu.VMEM((KEYS, width), bf16),
            pltpu.VMEM((PEERS, ROWS, BLOCK_COLS), bf16),
            pltpu.VMEM((PLACES, 2, PROMPT // PLACES, DH), bf16),
            pltpu.SemaphoreType.DMA((PEERS + 1,)),
            pltpu.SemaphoreType.DMA((PEERS + 1,)),
        ],
        compiler_params=pltpu.CompilerParams(vmem_limit_bytes=40 * 2**20),
        cost_estimate=pl.CostEstimate(
            flops=12 * PEERS * width * KEYS * DH,
            bytes_accessed=4 * 2**20,
            transcendentals=PEERS * width * KEYS,
        ),
        name="attend",
    )(me, lengths, prompt, *held)
    prompt_part = made[PEERS]

    moved = lax.all_to_all(prompt_part, ROW_AXES, split_axis=0, concat_axis=0, tiled=True)
    summed = jnp.sum(moved.astype(jnp.float32), axis=0)
    summed = summed.reshape(2, 16, own_rows, DH).transpose(1, 0, 2, 3)
    owned = lax.all_to_all(summed, Z_AXES, split_axis=0, concat_axis=0, tiled=True)
    owned = jnp.sum(owned.reshape(2, PEERS, 2, own_rows, DH), axis=0)
    owned = owned.transpose(1, 2, 0, 3).reshape(2, own_rows, PEERS * DH)

    back = exchange(made[:PEERS])
    results = pl.pallas_call(
        unpack_kernel,
        out_shape=[jax.ShapeDtypeStruct(a.shape, bf16) for a in (queries, queries, resp_keys, resp_values)],
        in_specs=[SMEM] + [ANY] * PEERS,
        out_specs=[ANY] * 4,
        scratch_shapes=[pltpu.SemaphoreType.DMA((4 * PEERS,))],
        name="unpack",
    )(me, *back)
    return (*results, owned[0], owned[1])


def solution(mesh):
    fine = Mesh(mesh.devices.reshape(8, 4, 2, 4, 2), AXES)
    rows = P(AXES, None)
    return jax.shard_map(
        on_device,
        mesh=fine,
        in_specs=(rows,) * 6 + (P(("y", "x", "z_hi"), None),),
        out_specs=(rows,) * 6,
        check_vma=False,
    )
```

```python
import functools
import math

import jax
import jax.numpy as jnp
from jax import lax
from jax.experimental import pallas as pl
from jax.experimental.pallas import tpu as pltpu
from jax.sharding import Mesh, PartitionSpec as P

DH = 128
AXES = ("y_hi", "y_lo", "x", "z_hi", "z_lo", "core")
FIRST_AXES = ("y_hi", "z_hi", "z_lo", "core")
HEAD_AXES = ("z_lo", "core")
PEERS = 8
SLOTS = 4
ROWS = 32
GROUP = 8
QCOLS = GROUP * DH
BLOCK_COLS = 2 * QCOLS + 2 * DH
OWN = PEERS * ROWS
FIRST = 32
XS = 4
XROWS = 256
PROMPT = XS * XROWS
KEYS = PROMPT + OWN
CHUNK = 256
STEP = 128
PAIR = 2
WIDTH = PAIR * GROUP * ROWS
FLOOR = -1e30
SCALE = 1.0 / math.sqrt(DH)
EXP2_SCALE = SCALE * math.log2(math.e)
ANY = pl.BlockSpec(memory_space=pl.ANY)
VMEM = pl.BlockSpec(memory_space=pltpu.VMEM)
SMEM = pl.BlockSpec(memory_space=pltpu.SMEM)


def cut_at(peer):
    wide, narrow = pl.ds(peer * QCOLS, QCOLS), pl.ds(peer * DH, DH)
    return (
        (wide, pl.ds(0, QCOLS)),
        (wide, pl.ds(QCOLS, QCOLS)),
        (narrow, pl.ds(2 * QCOLS, DH)),
        (narrow, pl.ds(2 * QCOLS + DH, DH)),
    )


def pack_kernel(q_ref, g_ref, k_ref, v_ref, out, sems):
    copies = []
    for peer in range(PEERS):
        for n, (src, (here, there)) in enumerate(zip((q_ref, g_ref, k_ref, v_ref), cut_at(peer))):
            copies.append(
                pltpu.make_async_copy(src.at[:, here], out.at[peer, :, there], sems.at[peer * 4 + n])
            )
    for copy in copies:
        copy.start()
    for copy in copies:
        copy.wait()


def unpack_kernel(blocks, *rest):
    outs, sems = rest[:4], rest[4]
    copies = []
    for peer in range(PEERS):
        for n, (dst, (here, there)) in enumerate(zip(outs, cut_at(peer))):
            copies.append(
                pltpu.make_async_copy(
                    blocks.at[peer, :, there], dst.at[:, here], sems.at[peer * 4 + n]
                )
            )
    for copy in copies:
        copy.start()
    for copy in copies:
        copy.wait()


def attend_kernel(len_ref, blocks, *rest):
    prompts, outs, prompt_outs, rest = rest[:XS], rest[XS], rest[XS + 1 : 2 * XS + 1], rest[2 * XS + 1 :]
    (
        held, held_kv, prompt_held, keys, values, keys_t, values_t,
        dkeys, dvalues, e_ref, p_ref, d_ref, made, made_kv, prompt_made, sems, out_sems,
    ) = rest
    heads, tail = pl.ds(0, 2 * QCOLS), pl.ds(2 * QCOLS, 2 * DH)
    first_in = [pltpu.make_async_copy(blocks.at[:, :, tail], held_kv, sems.at[PEERS])]
    for a in range(XS):
        first_in.append(pltpu.make_async_copy(prompts[a], prompt_held.at[a], sems.at[PEERS + 1 + a]))
    ins = [
        pltpu.make_async_copy(blocks.at[j, :, heads], held.at[j], sems.at[j]) for j in range(PEERS)
    ]
    for copy in first_in + ins:
        copy.start()
    for copy in first_in:
        copy.wait()
    for n, (natural, turned) in enumerate(((keys, keys_t), (values, values_t))):
        natural[:PROMPT, :] = prompt_held[:, :, n * DH : (n + 1) * DH].reshape(PROMPT, DH)
        natural[PROMPT:, :] = held_kv[:, :, n * DH : (n + 1) * DH].reshape(OWN, DH)
        for c in range(KEYS // CHUNK):
            turned[:, c * CHUNK : (c + 1) * CHUNK] = natural[c * CHUNK : (c + 1) * CHUNK, :].T
    ends = []
    total = jnp.int32(0)
    for n in range(SLOTS):
        total = total + len_ref[0, n]
        ends.append(total)
    lanes = lax.broadcasted_iota(jnp.int32, (1, WIDTH), 1)
    key_at = lax.broadcasted_iota(jnp.int32, (STEP, WIDTH), 0)
    chunks = [slice(c * CHUNK, (c + 1) * CHUNK) for c in range(KEYS // CHUNK)]
    steps = [slice(c * STEP, (c + 1) * STEP) for c in range(KEYS // STEP)]

    def stacked(s, base):
        return jnp.concatenate(
            [
                held[s + n, :, base + h * DH : base + (h + 1) * DH]
                for n in range(PAIR)
                for h in range(GROUP)
            ],
            axis=0,
        )

    outs_going = []
    for s in range(0, PEERS, PAIR):
        for n in range(PAIR):
            ins[s + n].wait()
        q, g = stacked(s, 0), stacked(s, QCOLS)
        q_t, g_t = q.T, g.T
        row = (s + lanes // (GROUP * ROWS)) * ROWS + lanes % ROWS
        start = jnp.zeros_like(row)
        for end in ends:
            start = jnp.maximum(start, jnp.where(end <= row, end, 0))
        peaks, sums = [], []
        for c in steps:
            x = jnp.dot(keys[c, :], q_t, preferred_element_type=jnp.float32)
            if c.start >= PROMPT:
                at = key_at + (c.start - PROMPT)
                x = jnp.where((at >= start) & (at <= row), x, -jnp.inf)
            peak = jnp.maximum(jnp.max(x, axis=0, keepdims=True), FLOOR) * EXP2_SCALE
            e = jnp.exp2(x * EXP2_SCALE - peak)
            e_ref[c, :] = e
            peaks.append(peak)
            sums.append(jnp.sum(e, axis=0, keepdims=True))
        top = functools.reduce(jnp.maximum, peaks)
        factors = [jnp.exp2(peak - top) for peak in peaks]
        inverse = 1.0 / sum(a * b for a, b in zip(factors, sums))
        factors = [factor * inverse for factor in factors]
        for c, factor in zip(steps, factors):
            p_ref[c, :] = (e_ref[c, :] * factor).astype(jnp.bfloat16)
        for c in chunks:
            part = jnp.dot(p_ref[c, :], g, preferred_element_type=jnp.float32)
            if s == 0:
                dvalues[c, :] = part
            else:
                dvalues[c, :] += part
        out_t = jnp.dot(values_t[...], p_ref[...], preferred_element_type=jnp.float32)
        out_t = out_t.astype(jnp.bfloat16)
        delta = jnp.sum(
            g_t.astype(jnp.float32) * out_t.astype(jnp.float32), axis=0, keepdims=True
        )
        for c, factor in zip(steps, factors):
            dw = jnp.dot(values[c, :], g_t, preferred_element_type=jnp.float32)
            d_ref[c, :] = ((e_ref[c, :] * factor) * (dw - delta)).astype(jnp.bfloat16)
        for c in chunks:
            part = jnp.dot(d_ref[c, :], q, preferred_element_type=jnp.float32)
            if s == 0:
                dkeys[c, :] = part
            else:
                dkeys[c, :] += part
        dq_t = jnp.dot(keys_t[...], d_ref[...], preferred_element_type=jnp.float32) * SCALE
        out = out_t.T
        dq = dq_t.astype(jnp.bfloat16).T
        for n in range(PAIR):
            for h in range(GROUP):
                at = slice((n * GROUP + h) * ROWS, (n * GROUP + h + 1) * ROWS)
                made[s + n, :, h * DH : (h + 1) * DH] = out[at, :]
                made[s + n, :, QCOLS + h * DH : QCOLS + (h + 1) * DH] = dq[at, :]
            copy = pltpu.make_async_copy(
                made.at[s + n], outs.at[s + n, :, heads], out_sems.at[s + n]
            )
            copy.start()
            outs_going.append(copy)
    for n, (grads, factor) in enumerate(((dkeys, SCALE), (dvalues, 1.0))):
        prompt_made[:, :, n * DH : (n + 1) * DH] = (
            (grads[:PROMPT, :] * factor).astype(jnp.bfloat16).reshape(XS, XROWS, DH)
        )
        made_kv[:, :, n * DH : (n + 1) * DH] = (
            (grads[PROMPT:, :] * factor).astype(jnp.bfloat16).reshape(PEERS, ROWS, DH)
        )
    backs = [pltpu.make_async_copy(made_kv, outs.at[:, :, tail], out_sems.at[PEERS])]
    for a in range(XS):
        backs.append(
            pltpu.make_async_copy(prompt_made.at[a], prompt_outs[a], out_sems.at[PEERS + 1 + a])
        )
    for copy in backs:
        copy.start()
    for copy in outs_going + backs:
        copy.wait()


def across(value, axis, s):
    n = lax.axis_size(axis)
    return lax.ppermute(value, axis, [(i, i ^ s) for i in range(n)])


def attend(lengths, held, prompt):
    bf16 = jnp.bfloat16
    block = jax.ShapeDtypeStruct((PEERS, ROWS, BLOCK_COLS), bf16)
    piece = jax.ShapeDtypeStruct((XROWS, 2 * DH), bf16)
    return pl.pallas_call(
        attend_kernel,
        out_shape=[block] + [piece] * XS,
        in_specs=[SMEM] + [ANY] * (XS + 1),
        out_specs=[ANY] * (XS + 1),
        scratch_shapes=[
            pltpu.VMEM((PEERS, ROWS, 2 * QCOLS), bf16),
            pltpu.VMEM((PEERS, ROWS, 2 * DH), bf16),
            pltpu.VMEM((XS, XROWS, 2 * DH), bf16),
            pltpu.VMEM((KEYS, DH), bf16),
            pltpu.VMEM((KEYS, DH), bf16),
            pltpu.VMEM((DH, KEYS), bf16),
            pltpu.VMEM((DH, KEYS), bf16),
            pltpu.VMEM((KEYS, DH), jnp.float32),
            pltpu.VMEM((KEYS, DH), jnp.float32),
            pltpu.VMEM((KEYS, WIDTH), jnp.float32),
            pltpu.VMEM((KEYS, WIDTH), bf16),
            pltpu.VMEM((KEYS, WIDTH), bf16),
            pltpu.VMEM((PEERS, ROWS, 2 * QCOLS), bf16),
            pltpu.VMEM((PEERS, ROWS, 2 * DH), bf16),
            pltpu.VMEM((XS, XROWS, 2 * DH), bf16),
            pltpu.SemaphoreType.DMA((PEERS + 1 + XS,)),
            pltpu.SemaphoreType.DMA((PEERS + 1 + XS,)),
        ],
        compiler_params=pltpu.CompilerParams(vmem_limit_bytes=40 * 2**20),
        cost_estimate=pl.CostEstimate(
            flops=12 * PEERS * GROUP * ROWS * KEYS * DH,
            bytes_accessed=4 * 2**20,
            transcendentals=PEERS * GROUP * ROWS * KEYS,
        ),
        name="attend",
    )(lengths, held, *prompt)


def on_device(queries, resp_keys, resp_values, out_grad, prompt_keys, prompt_values, lengths):
    bf16, f32 = jnp.bfloat16, jnp.float32
    own_rows = prompt_keys.shape[0]

    by_head = jnp.concatenate(
        [prompt_keys.reshape(own_rows, PEERS, DH), prompt_values.reshape(own_rows, PEERS, DH)], axis=2
    ).transpose(1, 0, 2)
    by_head = jnp.broadcast_to(by_head[None], (4,) + by_head.shape).reshape(FIRST, own_rows, 2 * DH)
    line = lax.all_to_all(by_head, FIRST_AXES, split_axis=0, concat_axis=0, tiled=True)

    packed = pl.pallas_call(
        pack_kernel,
        out_shape=jax.ShapeDtypeStruct((PEERS, ROWS, BLOCK_COLS), bf16),
        in_specs=[ANY] * 4,
        out_specs=VMEM,
        scratch_shapes=[pltpu.SemaphoreType.DMA((4 * PEERS,))],
        name="pack",
    )(queries, out_grad, resp_keys, resp_values)
    line, packed = lax.optimization_barrier((line, packed))
    held = lax.all_to_all(packed, HEAD_AXES, split_axis=0, concat_axis=0, tiled=True)

    line = line.reshape(FIRST * own_rows, 2 * DH)
    line = jnp.concatenate([line] + [across(line, "y_lo", b) for b in (1, 2, 3)], axis=0)
    prompt = [line] + [across(line, "x", a) for a in (1, 2, 3)]

    made, *parts = attend(lengths, held, prompt)

    back = lax.all_to_all(made, HEAD_AXES, split_axis=0, concat_axis=0, tiled=True)

    total = parts[0].astype(f32)
    for a in (1, 2, 3):
        total = total + across(parts[a], "x", a).astype(f32)
    total = total.astype(bf16).reshape(4, XROWS // 4, 2 * DH)
    pieces = [total[b] for b in range(4)]
    total = pieces[0].astype(f32)
    for b in (1, 2, 3):
        total = total + across(pieces[b], "y_lo", b).astype(f32)
    total, back = lax.optimization_barrier((total, back))
    owned = lax.all_to_all(
        total.reshape(FIRST, own_rows, 2 * DH), FIRST_AXES, split_axis=0, concat_axis=0, tiled=True
    )
    owned = jnp.sum(owned.reshape(4, PEERS, own_rows, 2, DH), axis=0)
    owned = owned.transpose(2, 1, 0, 3).reshape(2, own_rows, PEERS * DH)

    results = pl.pallas_call(
        unpack_kernel,
        out_shape=[jax.ShapeDtypeStruct(a.shape, bf16) for a in (queries, queries, resp_keys, resp_values)],
        in_specs=[ANY],
        out_specs=[VMEM] * 4,
        scratch_shapes=[pltpu.SemaphoreType.DMA((4 * PEERS,))],
        name="unpack",
    )(back)
    return (*results, owned[0], owned[1])


def solution(mesh):
    fine = Mesh(mesh.devices.reshape(2, 4, 4, 2, 4, 2), AXES)
    rows = P(AXES, None)
    return jax.shard_map(
        on_device,
        mesh=fine,
        in_specs=(rows,) * 6 + (P(("y_hi", "y_lo", "x", "z_hi"), None),),
        out_specs=(rows,) * 6,
        check_vma=False,
    )
```

```python
import functools
import math

import jax
import jax.numpy as jnp
from jax import lax
from jax.experimental import pallas as pl
from jax.experimental.pallas import tpu as pltpu
from jax.sharding import Mesh, PartitionSpec as P

DH = 128
AXES = ("y_lo", "y_hi", "x", "z_hi", "z_lo", "core")
FIRST_AXES = ("y_hi", "z_hi", "z_lo", "core")
HEAD_AXES = ("z_lo", "core")
PEERS = 8
SLOTS = 4
ROWS = 32
GROUP = 8
QCOLS = GROUP * DH
BLOCK_COLS = 2 * QCOLS + 2 * DH
OWN = PEERS * ROWS
FIRST = 32
XS = 4
XROWS = 256
PROMPT = XS * XROWS
KEYS = PROMPT + OWN
CHUNK = 256
STEP = 128
PAIR = 2
WIDTH = PAIR * GROUP * ROWS
FLOOR = -1e30
SCALE = 1.0 / math.sqrt(DH)
EXP2_SCALE = SCALE * math.log2(math.e)
ANY = pl.BlockSpec(memory_space=pl.ANY)
VMEM = pl.BlockSpec(memory_space=pltpu.VMEM)
SMEM = pl.BlockSpec(memory_space=pltpu.SMEM)


def cut_at(peer):
    wide, narrow = pl.ds(peer * QCOLS, QCOLS), pl.ds(peer * DH, DH)
    return (
        (wide, pl.ds(0, QCOLS)),
        (wide, pl.ds(QCOLS, QCOLS)),
        (narrow, pl.ds(2 * QCOLS, DH)),
        (narrow, pl.ds(2 * QCOLS + DH, DH)),
    )


def pack_kernel(q_ref, g_ref, k_ref, v_ref, out, sems):
    copies = []
    for peer in range(PEERS):
        for n, (src, (here, there)) in enumerate(zip((q_ref, g_ref, k_ref, v_ref), cut_at(peer))):
            copies.append(
                pltpu.make_async_copy(src.at[:, here], out.at[peer, :, there], sems.at[peer * 4 + n])
            )
    for copy in copies:
        copy.start()
    for copy in copies:
        copy.wait()


def unpack_kernel(blocks, *rest):
    outs, sems = rest[:4], rest[4]
    copies = []
    for peer in range(PEERS):
        for n, (dst, (here, there)) in enumerate(zip(outs, cut_at(peer))):
            copies.append(
                pltpu.make_async_copy(
                    blocks.at[peer, :, there], dst.at[:, here], sems.at[peer * 4 + n]
                )
            )
    for copy in copies:
        copy.start()
    for copy in copies:
        copy.wait()


def attend_kernel(len_ref, blocks, *rest):
    prompts, outs, prompt_outs, rest = rest[:XS], rest[XS], rest[XS + 1 : 2 * XS + 1], rest[2 * XS + 1 :]
    (
        held, held_kv, prompt_held, keys, values, keys_t, values_t,
        dkeys, dvalues, e_ref, p_ref, d_ref, made, made_kv, prompt_made, sems, out_sems,
    ) = rest
    heads, tail = pl.ds(0, 2 * QCOLS), pl.ds(2 * QCOLS, 2 * DH)
    first_in = [pltpu.make_async_copy(blocks.at[:, :, tail], held_kv, sems.at[PEERS])]
    for a in range(XS):
        first_in.append(pltpu.make_async_copy(prompts[a], prompt_held.at[a], sems.at[PEERS + 1 + a]))
    ins = [
        pltpu.make_async_copy(blocks.at[j, :, heads], held.at[j], sems.at[j]) for j in range(PEERS)
    ]
    for copy in first_in + ins:
        copy.start()
    for copy in first_in:
        copy.wait()
    for n, (natural, turned) in enumerate(((keys, keys_t), (values, values_t))):
        natural[:PROMPT, :] = prompt_held[:, :, n * DH : (n + 1) * DH].reshape(PROMPT, DH)
        natural[PROMPT:, :] = held_kv[:, :, n * DH : (n + 1) * DH].reshape(OWN, DH)
        for c in range(KEYS // CHUNK):
            turned[:, c * CHUNK : (c + 1) * CHUNK] = natural[c * CHUNK : (c + 1) * CHUNK, :].T
    ends = []
    total = jnp.int32(0)
    for n in range(SLOTS):
        total = total + len_ref[0, n]
        ends.append(total)
    lanes = lax.broadcasted_iota(jnp.int32, (1, WIDTH), 1)
    key_at = lax.broadcasted_iota(jnp.int32, (STEP, WIDTH), 0)
    steps = [slice(c * STEP, (c + 1) * STEP) for c in range(KEYS // STEP)]

    def stacked(s, base):
        return jnp.concatenate(
            [
                held[s + n, :, base + h * DH : base + (h + 1) * DH]
                for n in range(PAIR)
                for h in range(GROUP)
            ],
            axis=0,
        )

    outs_going = []
    for s in range(0, PEERS, PAIR):
        for n in range(PAIR):
            ins[s + n].wait()
        q, g = stacked(s, 0), stacked(s, QCOLS)
        q_t, g_t = q.T, g.T
        row = (s + lanes // (GROUP * ROWS)) * ROWS + lanes % ROWS
        start = jnp.zeros_like(row)
        for end in ends:
            start = jnp.maximum(start, jnp.where(end <= row, end, 0))
        peaks, sums = [], []
        for c in steps:
            x = jnp.dot(keys[c, :], q_t, preferred_element_type=jnp.float32)
            if c.start >= PROMPT:
                at = key_at + (c.start - PROMPT)
                x = jnp.where((at >= start) & (at <= row), x, -jnp.inf)
            peak = jnp.maximum(jnp.max(x, axis=0, keepdims=True), FLOOR) * EXP2_SCALE
            e = jnp.exp2(x * EXP2_SCALE - peak)
            e_ref[c, :] = e
            peaks.append(peak)
            sums.append(jnp.sum(e, axis=0, keepdims=True))
        top = functools.reduce(jnp.maximum, peaks)
        factors = [jnp.exp2(peak - top) for peak in peaks]
        inverse = 1.0 / sum(a * b for a, b in zip(factors, sums))
        factors = [factor * inverse for factor in factors]
        for c, factor in zip(steps, factors):
            p_ref[c, :] = (e_ref[c, :] * factor).astype(jnp.bfloat16)
        part = jnp.dot(p_ref[...], g, preferred_element_type=jnp.float32)
        if s == 0:
            dvalues[...] = part
        else:
            dvalues[...] += part
        out_t = jnp.dot(values_t[...], p_ref[...], preferred_element_type=jnp.float32)
        out_t = out_t.astype(jnp.bfloat16)
        delta = jnp.sum(
            g_t.astype(jnp.float32) * out_t.astype(jnp.float32), axis=0, keepdims=True
        )
        for c, factor in zip(steps, factors):
            dw = jnp.dot(values[c, :], g_t, preferred_element_type=jnp.float32)
            d_ref[c, :] = ((e_ref[c, :] * factor) * (dw - delta)).astype(jnp.bfloat16)
        part = jnp.dot(d_ref[...], q, preferred_element_type=jnp.float32)
        if s == 0:
            dkeys[...] = part
        else:
            dkeys[...] += part
        dq_t = jnp.dot(keys_t[...], d_ref[...], preferred_element_type=jnp.float32) * SCALE
        out = out_t.T
        dq = dq_t.astype(jnp.bfloat16).T
        for n in range(PAIR):
            for h in range(GROUP):
                at = slice((n * GROUP + h) * ROWS, (n * GROUP + h + 1) * ROWS)
                made[s + n, :, h * DH : (h + 1) * DH] = out[at, :]
                made[s + n, :, QCOLS + h * DH : QCOLS + (h + 1) * DH] = dq[at, :]
            copy = pltpu.make_async_copy(
                made.at[s + n], outs.at[s + n, :, heads], out_sems.at[s + n]
            )
            copy.start()
            outs_going.append(copy)
    for n, (grads, factor) in enumerate(((dkeys, SCALE), (dvalues, 1.0))):
        prompt_made[:, :, n * DH : (n + 1) * DH] = (
            (grads[:PROMPT, :] * factor).astype(jnp.bfloat16).reshape(XS, XROWS, DH)
        )
        made_kv[:, :, n * DH : (n + 1) * DH] = (
            (grads[PROMPT:, :] * factor).astype(jnp.bfloat16).reshape(PEERS, ROWS, DH)
        )
    backs = [pltpu.make_async_copy(made_kv, outs.at[:, :, tail], out_sems.at[PEERS])]
    for a in range(XS):
        backs.append(
            pltpu.make_async_copy(prompt_made.at[a], prompt_outs[a], out_sems.at[PEERS + 1 + a])
        )
    for copy in backs:
        copy.start()
    for copy in outs_going + backs:
        copy.wait()


def across(value, axis, s):
    n = lax.axis_size(axis)
    return lax.ppermute(value, axis, [(i, i ^ s) for i in range(n)])


def attend(lengths, held, prompt):
    bf16 = jnp.bfloat16
    block = jax.ShapeDtypeStruct((PEERS, ROWS, BLOCK_COLS), bf16)
    piece = jax.ShapeDtypeStruct((XROWS, 2 * DH), bf16)
    return pl.pallas_call(
        attend_kernel,
        out_shape=[block] + [piece] * XS,
        in_specs=[SMEM] + [ANY] * (XS + 1),
        out_specs=[ANY] * (XS + 1),
        scratch_shapes=[
            pltpu.VMEM((PEERS, ROWS, 2 * QCOLS), bf16),
            pltpu.VMEM((PEERS, ROWS, 2 * DH), bf16),
            pltpu.VMEM((XS, XROWS, 2 * DH), bf16),
            pltpu.VMEM((KEYS, DH), bf16),
            pltpu.VMEM((KEYS, DH), bf16),
            pltpu.VMEM((DH, KEYS), bf16),
            pltpu.VMEM((DH, KEYS), bf16),
            pltpu.VMEM((KEYS, DH), jnp.float32),
            pltpu.VMEM((KEYS, DH), jnp.float32),
            pltpu.VMEM((KEYS, WIDTH), jnp.float32),
            pltpu.VMEM((KEYS, WIDTH), bf16),
            pltpu.VMEM((KEYS, WIDTH), bf16),
            pltpu.VMEM((PEERS, ROWS, 2 * QCOLS), bf16),
            pltpu.VMEM((PEERS, ROWS, 2 * DH), bf16),
            pltpu.VMEM((XS, XROWS, 2 * DH), bf16),
            pltpu.SemaphoreType.DMA((PEERS + 1 + XS,)),
            pltpu.SemaphoreType.DMA((PEERS + 1 + XS,)),
        ],
        compiler_params=pltpu.CompilerParams(vmem_limit_bytes=40 * 2**20),
        cost_estimate=pl.CostEstimate(
            flops=12 * PEERS * GROUP * ROWS * KEYS * DH,
            bytes_accessed=4 * 2**20,
            transcendentals=PEERS * GROUP * ROWS * KEYS,
        ),
        name="attend",
    )(lengths, held, *prompt)


def on_device(queries, resp_keys, resp_values, out_grad, prompt_keys, prompt_values, lengths):
    bf16, f32 = jnp.bfloat16, jnp.float32
    own_rows = prompt_keys.shape[0]

    by_head = jnp.concatenate(
        [prompt_keys.reshape(own_rows, PEERS, DH), prompt_values.reshape(own_rows, PEERS, DH)], axis=2
    ).transpose(1, 0, 2)
    by_head = jnp.broadcast_to(by_head[None], (4,) + by_head.shape).reshape(FIRST, own_rows, 2 * DH)
    line = lax.all_to_all(by_head, FIRST_AXES, split_axis=0, concat_axis=0, tiled=True)

    packed = pl.pallas_call(
        pack_kernel,
        out_shape=jax.ShapeDtypeStruct((PEERS, ROWS, BLOCK_COLS), bf16),
        in_specs=[ANY] * 4,
        out_specs=VMEM,
        scratch_shapes=[pltpu.SemaphoreType.DMA((4 * PEERS,))],
        name="pack",
    )(queries, out_grad, resp_keys, resp_values)
    line, packed = lax.optimization_barrier((line, packed))
    held = lax.all_to_all(packed, HEAD_AXES, split_axis=0, concat_axis=0, tiled=True)

    line = line.reshape(FIRST * own_rows, 2 * DH)
    line = jnp.concatenate([line] + [across(line, "y_lo", b) for b in (1, 2, 3)], axis=0)
    prompt = [line] + [across(line, "x", a) for a in (1, 2, 3)]

    made, *parts = attend(lengths, held, prompt)

    back = lax.all_to_all(made, HEAD_AXES, split_axis=0, concat_axis=0, tiled=True)

    total = parts[0].astype(f32)
    for a in (1, 2, 3):
        total = total + across(parts[a], "x", a).astype(f32)
    total = total.astype(bf16).reshape(4, XROWS // 4, 2 * DH)
    pieces = [total[b] for b in range(4)]
    total = pieces[0].astype(f32)
    for b in (1, 2, 3):
        total = total + across(pieces[b], "y_lo", b).astype(f32)
    total, back = lax.optimization_barrier((total.reshape(FIRST, own_rows, 2 * DH), back))
    owned = lax.all_to_all(total, FIRST_AXES, split_axis=0, concat_axis=0, tiled=True)
    owned = jnp.sum(owned.reshape(4, PEERS, own_rows, 2, DH), axis=0)
    owned = owned.transpose(2, 1, 0, 3).reshape(2, own_rows, PEERS * DH)

    results = pl.pallas_call(
        unpack_kernel,
        out_shape=[jax.ShapeDtypeStruct(a.shape, bf16) for a in (queries, queries, resp_keys, resp_values)],
        in_specs=[ANY],
        out_specs=[VMEM] * 4,
        scratch_shapes=[pltpu.SemaphoreType.DMA((4 * PEERS,))],
        name="unpack",
    )(back)
    return (*results, owned[0], owned[1])


def solution(mesh):
    fine = Mesh(mesh.devices.reshape(4, 2, 4, 2, 4, 2), AXES)
    rows = P(AXES, None)
    return jax.shard_map(
        on_device,
        mesh=fine,
        in_specs=(rows,) * 6 + (P(("y_lo", "y_hi", "x", "z_hi"), None),),
        out_specs=(rows,) * 6,
        check_vma=False,
    )
```

```python
import functools
import math

import jax
import jax.numpy as jnp
from jax import lax
from jax.experimental import pallas as pl
from jax.experimental.pallas import tpu as pltpu
from jax.sharding import Mesh, PartitionSpec as P

DH = 128
AXES = ("y4", "y2", "y1", "x", "z_hi", "z_lo", "core")
RESP_AXES = ("y4", "y2", "y1", "x", "z_hi")
FIRST_AXES = ("y1", "z_hi", "z_lo", "core")
LAST_AXES = ("y2",) + FIRST_AXES
HEAD_AXES = ("z_lo", "core")
PEERS = 8
SLOTS = 4
ROWS = 32
GROUP = 8
QCOLS = GROUP * DH
BLOCK_COLS = 2 * QCOLS + 2 * DH
OWN = PEERS * ROWS
FIRST = 32
LAST = 64
XS = 4
XROWS = 256
PROMPT = XS * XROWS
KEYS = PROMPT + OWN
CHUNK = 256
STEP = 128
PAIR = 2
WIDTH = PAIR * GROUP * ROWS
FLOOR = -1e30
SCALE = 1.0 / math.sqrt(DH)
EXP2_SCALE = SCALE * math.log2(math.e)
ANY = pl.BlockSpec(memory_space=pl.ANY)
VMEM = pl.BlockSpec(memory_space=pltpu.VMEM)
SMEM = pl.BlockSpec(memory_space=pltpu.SMEM)


def cut_at(peer):
    wide, narrow = pl.ds(peer * QCOLS, QCOLS), pl.ds(peer * DH, DH)
    return (
        (wide, pl.ds(0, QCOLS)),
        (wide, pl.ds(QCOLS, QCOLS)),
        (narrow, pl.ds(2 * QCOLS, DH)),
        (narrow, pl.ds(2 * QCOLS + DH, DH)),
    )


def pack_kernel(q_ref, g_ref, k_ref, v_ref, out, sems):
    copies = []
    for peer in range(PEERS):
        for n, (src, (here, there)) in enumerate(zip((q_ref, g_ref, k_ref, v_ref), cut_at(peer))):
            copies.append(
                pltpu.make_async_copy(src.at[:, here], out.at[peer, :, there], sems.at[peer * 4 + n])
            )
    for copy in copies:
        copy.start()
    for copy in copies:
        copy.wait()


def unpack_kernel(blocks, *rest):
    outs, sems = rest[:4], rest[4]
    copies = []
    for peer in range(PEERS):
        for n, (dst, (here, there)) in enumerate(zip(outs, cut_at(peer))):
            copies.append(
                pltpu.make_async_copy(
                    blocks.at[peer, :, there], dst.at[:, here], sems.at[peer * 4 + n]
                )
            )
    for copy in copies:
        copy.start()
    for copy in copies:
        copy.wait()


def attend_kernel(len_ref, blocks, *rest):
    prompts, outs, prompt_outs, rest = rest[:XS], rest[XS], rest[XS + 1 : 2 * XS + 1], rest[2 * XS + 1 :]
    (
        held, held_kv, prompt_held, keys, values, keys_t, values_t,
        dkeys, dvalues, e_ref, p_ref, d_ref, made, made_kv, prompt_made, sems, out_sems,
    ) = rest
    heads, tail = pl.ds(0, 2 * QCOLS), pl.ds(2 * QCOLS, 2 * DH)
    first_in = [pltpu.make_async_copy(blocks.at[:, :, tail], held_kv, sems.at[PEERS])]
    for a in range(XS):
        first_in.append(pltpu.make_async_copy(prompts[a], prompt_held.at[a], sems.at[PEERS + 1 + a]))
    ins = [
        pltpu.make_async_copy(blocks.at[j, :, heads], held.at[j], sems.at[j]) for j in range(PEERS)
    ]
    for copy in first_in + ins:
        copy.start()
    for copy in first_in:
        copy.wait()
    for n, (natural, turned) in enumerate(((keys, keys_t), (values, values_t))):
        natural[:PROMPT, :] = prompt_held[:, :, n * DH : (n + 1) * DH].reshape(PROMPT, DH)
        natural[PROMPT:, :] = held_kv[:, :, n * DH : (n + 1) * DH].reshape(OWN, DH)
        for c in range(KEYS // CHUNK):
            turned[:, c * CHUNK : (c + 1) * CHUNK] = natural[c * CHUNK : (c + 1) * CHUNK, :].T
    ends = []
    total = jnp.int32(0)
    for n in range(SLOTS):
        total = total + len_ref[0, n]
        ends.append(total)
    lanes = lax.broadcasted_iota(jnp.int32, (1, WIDTH), 1)
    key_at = lax.broadcasted_iota(jnp.int32, (STEP, WIDTH), 0)
    steps = [slice(c * STEP, (c + 1) * STEP) for c in range(KEYS // STEP)]

    def stacked(s, base):
        return jnp.concatenate(
            [
                held[s + n, :, base + h * DH : base + (h + 1) * DH]
                for n in range(PAIR)
                for h in range(GROUP)
            ],
            axis=0,
        )

    outs_going = []
    for s in range(0, PEERS, PAIR):
        for n in range(PAIR):
            ins[s + n].wait()
        q, g = stacked(s, 0), stacked(s, QCOLS)
        q_t, g_t = q.T, g.T
        row = (s + lanes // (GROUP * ROWS)) * ROWS + lanes % ROWS
        start = jnp.zeros_like(row)
        for end in ends:
            start = jnp.maximum(start, jnp.where(end <= row, end, 0))
        peaks, sums = [], []
        for c in steps:
            x = jnp.dot(keys[c, :], q_t, preferred_element_type=jnp.float32)
            if c.start >= PROMPT:
                at = key_at + (c.start - PROMPT)
                x = jnp.where((at >= start) & (at <= row), x, -jnp.inf)
            peak = jnp.maximum(jnp.max(x, axis=0, keepdims=True), FLOOR) * EXP2_SCALE
            e = jnp.exp2(x * EXP2_SCALE - peak)
            e_ref[c, :] = e
            peaks.append(peak)
            sums.append(jnp.sum(e, axis=0, keepdims=True))
        top = functools.reduce(jnp.maximum, peaks)
        factors = [jnp.exp2(peak - top) for peak in peaks]
        inverse = 1.0 / sum(a * b for a, b in zip(factors, sums))
        factors = [factor * inverse for factor in factors]
        for c, factor in zip(steps, factors):
            p_ref[c, :] = (e_ref[c, :] * factor).astype(jnp.bfloat16)
        part = jnp.dot(p_ref[...], g, preferred_element_type=jnp.float32)
        if s == 0:
            dvalues[...] = part
        else:
            dvalues[...] += part
        out_t = jnp.dot(values_t[...], p_ref[...], preferred_element_type=jnp.float32)
        out_t = out_t.astype(jnp.bfloat16)
        delta = jnp.sum(
            g_t.astype(jnp.float32) * out_t.astype(jnp.float32), axis=0, keepdims=True
        )
        for c, factor in zip(steps, factors):
            dw = jnp.dot(values[c, :], g_t, preferred_element_type=jnp.float32)
            d_ref[c, :] = ((e_ref[c, :] * factor) * (dw - delta)).astype(jnp.bfloat16)
        part = jnp.dot(d_ref[...], q, preferred_element_type=jnp.float32)
        if s == 0:
            dkeys[...] = part
        else:
            dkeys[...] += part
        dq_t = jnp.dot(keys_t[...], d_ref[...], preferred_element_type=jnp.float32) * SCALE
        out = out_t.T
        dq = dq_t.astype(jnp.bfloat16).T
        for n in range(PAIR):
            for h in range(GROUP):
                at = slice((n * GROUP + h) * ROWS, (n * GROUP + h + 1) * ROWS)
                made[s + n, :, h * DH : (h + 1) * DH] = out[at, :]
                made[s + n, :, QCOLS + h * DH : QCOLS + (h + 1) * DH] = dq[at, :]
            copy = pltpu.make_async_copy(
                made.at[s + n], outs.at[s + n, :, heads], out_sems.at[s + n]
            )
            copy.start()
            outs_going.append(copy)
    for n, (grads, factor) in enumerate(((dkeys, SCALE), (dvalues, 1.0))):
        prompt_made[:, :, n * DH : (n + 1) * DH] = (
            (grads[:PROMPT, :] * factor).astype(jnp.bfloat16).reshape(XS, XROWS, DH)
        )
        made_kv[:, :, n * DH : (n + 1) * DH] = (
            (grads[PROMPT:, :] * factor).astype(jnp.bfloat16).reshape(PEERS, ROWS, DH)
        )
    backs = [pltpu.make_async_copy(made_kv, outs.at[:, :, tail], out_sems.at[PEERS])]
    for a in range(XS):
        backs.append(
            pltpu.make_async_copy(prompt_made.at[a], prompt_outs[a], out_sems.at[PEERS + 1 + a])
        )
    for copy in backs:
        copy.start()
    for copy in outs_going + backs:
        copy.wait()


def across(value, axis, s):
    n = lax.axis_size(axis)
    return lax.ppermute(value, axis, [(i, i ^ s) for i in range(n)])


def attend(lengths, held, prompt):
    bf16 = jnp.bfloat16
    block = jax.ShapeDtypeStruct((PEERS, ROWS, BLOCK_COLS), bf16)
    piece = jax.ShapeDtypeStruct((XROWS, 2 * DH), bf16)
    return pl.pallas_call(
        attend_kernel,
        out_shape=[block] + [piece] * XS,
        in_specs=[SMEM] + [ANY] * (XS + 1),
        out_specs=[ANY] * (XS + 1),
        scratch_shapes=[
            pltpu.VMEM((PEERS, ROWS, 2 * QCOLS), bf16),
            pltpu.VMEM((PEERS, ROWS, 2 * DH), bf16),
            pltpu.VMEM((XS, XROWS, 2 * DH), bf16),
            pltpu.VMEM((KEYS, DH), bf16),
            pltpu.VMEM((KEYS, DH), bf16),
            pltpu.VMEM((DH, KEYS), bf16),
            pltpu.VMEM((DH, KEYS), bf16),
            pltpu.VMEM((KEYS, DH), jnp.float32),
            pltpu.VMEM((KEYS, DH), jnp.float32),
            pltpu.VMEM((KEYS, WIDTH), jnp.float32),
            pltpu.VMEM((KEYS, WIDTH), bf16),
            pltpu.VMEM((KEYS, WIDTH), bf16),
            pltpu.VMEM((PEERS, ROWS, 2 * QCOLS), bf16),
            pltpu.VMEM((PEERS, ROWS, 2 * DH), bf16),
            pltpu.VMEM((XS, XROWS, 2 * DH), bf16),
            pltpu.SemaphoreType.DMA((PEERS + 1 + XS,)),
            pltpu.SemaphoreType.DMA((PEERS + 1 + XS,)),
        ],
        compiler_params=pltpu.CompilerParams(vmem_limit_bytes=40 * 2**20),
        cost_estimate=pl.CostEstimate(
            flops=12 * PEERS * GROUP * ROWS * KEYS * DH,
            bytes_accessed=4 * 2**20,
            transcendentals=PEERS * GROUP * ROWS * KEYS,
        ),
        name="attend",
    )(lengths, held, *prompt)


def on_device(queries, resp_keys, resp_values, out_grad, prompt_keys, prompt_values, lengths):
    bf16, f32 = jnp.bfloat16, jnp.float32
    own_rows = prompt_keys.shape[0]

    by_head = jnp.concatenate(
        [prompt_keys.reshape(own_rows, PEERS, DH), prompt_values.reshape(own_rows, PEERS, DH)], axis=2
    ).transpose(1, 0, 2)
    by_head = jnp.broadcast_to(by_head[None], (4,) + by_head.shape).reshape(FIRST, own_rows, 2 * DH)
    line = lax.all_to_all(by_head, FIRST_AXES, split_axis=0, concat_axis=0, tiled=True)

    packed = pl.pallas_call(
        pack_kernel,
        out_shape=jax.ShapeDtypeStruct((PEERS, ROWS, BLOCK_COLS), bf16),
        in_specs=[ANY] * 4,
        out_specs=VMEM,
        scratch_shapes=[pltpu.SemaphoreType.DMA((4 * PEERS,))],
        name="pack",
    )(queries, out_grad, resp_keys, resp_values)
    line, packed = lax.optimization_barrier((line, packed))
    held = lax.all_to_all(packed, HEAD_AXES, split_axis=0, concat_axis=0, tiled=True)

    line = line.reshape(FIRST * own_rows, 2 * DH)
    for axis in ("y4", "y2"):
        line = jnp.concatenate([line, across(line, axis, 1)], axis=0)
    prompt = [line] + [across(line, "x", a) for a in (1, 2, 3)]

    made, *parts = attend(lengths, held, prompt)

    back = lax.all_to_all(made, HEAD_AXES, split_axis=0, concat_axis=0, tiled=True)

    total = parts[0].astype(f32)
    for a in (1, 2, 3):
        total = total + across(parts[a], "x", a).astype(f32)
    total = total.astype(bf16).reshape(2, 2, XROWS // 4, 2 * DH)
    total = total[:, 0].astype(f32) + across(total[:, 1], "y4", 1).astype(f32)
    total = jnp.where(lax.axis_index("y2") == 0, total, total[::-1])
    total, back = lax.optimization_barrier((total.reshape(LAST, own_rows, 2 * DH), back))
    owned = lax.all_to_all(total, LAST_AXES, split_axis=0, concat_axis=0, tiled=True)
    owned = jnp.sum(owned.reshape(LAST // PEERS, PEERS, own_rows, 2, DH), axis=0)
    owned = owned.transpose(2, 1, 0, 3).reshape(2, own_rows, PEERS * DH)

    results = pl.pallas_call(
        unpack_kernel,
        out_shape=[jax.ShapeDtypeStruct(a.shape, bf16) for a in (queries, queries, resp_keys, resp_values)],
        in_specs=[ANY],
        out_specs=[VMEM] * 4,
        scratch_shapes=[pltpu.SemaphoreType.DMA((4 * PEERS,))],
        name="unpack",
    )(back)
    return (*results, owned[0], owned[1])


def solution(mesh):
    fine = Mesh(mesh.devices.reshape(2, 2, 2, 4, 2, 4, 2), AXES)
    rows = P(AXES, None)
    return jax.shard_map(
        on_device,
        mesh=fine,
        in_specs=(rows,) * 6 + (P(RESP_AXES, None),),
        out_specs=(rows,) * 6,
        check_vma=False,
    )
```
